32 devices in a mesh: node: 8 (over y, x, core), local: 4 (over z).
Axes of the slice: x: 2, y: 2, z: 4, core: 2. Of those that a mesh axis runs over, the one named last changes fastest.
Arguments:
- expert_ids: int32 [4096, 4], P(('node', 'local')), may hold values from 0 to 31, as said below
- gate_weights: bfloat16 [4096, 4], P(('node', 'local')), may hold values from 0.099609375 to 1
- tokens_in: bfloat16 [4096, 3584], P(('node', 'local')), may hold values from -6 to 6
- grad_out: bfloat16 [4096, 3584], P(('node', 'local')), may hold values from -6 to 6
- w_gate: bfloat16 [32, 3584, 1024], P(('node', 'local')), may hold values from -0.09375 to 0.09375
- w_up: bfloat16 [32, 3584, 1024], P(('node', 'local')), may hold values from -0.09375 to 0.09375
- w_down: bfloat16 [32, 1024, 3584], P(('node', 'local')), may hold values from -0.1875 to 0.1875
Outputs:
- grad_in: bfloat16 [4096, 3584], P(('node', 'local'))
The draws below stay inside these ranges and needn't reach their ends.
Inputs may be any that keep to these rules, and one draw needn't show every extreme that they name: `expert_ids`: each token names 4 different experts, two in each of two different node groups; node group m holds experts 4 m to 4 m + 3. The tokens of one device pick every node group exactly 32 times. From the tokens of one device every expert gets at most 24 rows; in every node group one expert gets exactly 24 rows from every device, the others fewer, and every expert gets some rows.
All inputs are finite; a program needn't handle non-finite values.
Results may differ from the reference program's by a relative error of at most 0.0064.
Values may be sent and summed in bfloat16 or wider, within the bound.
No kernel may reach another device: no remote copies, remote signals or barrier semaphores. Data moves between devices by JAX's collectives and lax.ppermute only.
A program may use at most 128 MiB of HBM per device.

```python
import jax
import jax.numpy as jnp
from jax import lax

D = 3584
FF = 1024
TOK_DEV = 128
TOP = 4
EXPERTS = 32
TOKENS = 4096
VISITS = 32
SLOTS = 24
N_NODE = 8
N_LOCAL = 4


def draw_expert_ids(key, part):
    blocks = TOKENS // TOK_DEV
    rounds = TOK_DEV // N_NODE
    key_perm, key_shift, key_visit, key_hot, key_order = jax.random.split(key, 5)
    perm_keys = jax.random.split(key_perm, blocks * rounds)
    node_perms = jax.vmap(lambda subkey: jax.random.permutation(subkey, N_NODE))(perm_keys)
    node_perms = node_perms.reshape(blocks, rounds, N_NODE).astype(jnp.int32)
    shifts = jax.random.randint(key_shift, (blocks, rounds, 1), 1, N_NODE).astype(jnp.int32)
    positions = jnp.arange(N_NODE, dtype=jnp.int32)
    node_first = node_perms.reshape(blocks, TOK_DEV)
    node_second = jnp.take_along_axis(node_perms, (positions[None, None, :] + shifts) % N_NODE, axis=2).reshape(blocks, TOK_DEV)
    picks = ((node_first[..., None] == positions) | (node_second[..., None] == positions)).astype(jnp.int32)
    before = jnp.cumsum(picks, axis=1) - picks
    visit_first = jnp.take_along_axis(before, node_first[..., None], axis=2)[..., 0]
    visit_second = jnp.take_along_axis(before, node_second[..., None], axis=2)[..., 0]
    visit_keys = jax.random.split(key_visit, blocks * N_NODE)
    visit_perms = jax.vmap(lambda subkey: jax.random.permutation(subkey, VISITS))(visit_keys)
    visit_perms = visit_perms.reshape(blocks, N_NODE * VISITS).astype(jnp.int32)
    pattern_first = jnp.take_along_axis(visit_perms, node_first * VISITS + visit_first, axis=1)
    pattern_second = jnp.take_along_axis(visit_perms, node_second * VISITS + visit_second, axis=1)
    hot_local = jax.random.randint(key_hot, (N_NODE,), 0, N_LOCAL).astype(jnp.int32)

    def choose(node_pick, pattern):
        hot_pick = hot_local[node_pick]
        step_mod = pattern % 3
        with_hot = pattern < 3 * VISITS // 4
        other_one = (hot_pick + 1 + step_mod) % N_LOCAL
        other_two = (hot_pick + 1 + (step_mod + 1) % 3) % N_LOCAL
        first_pick = jnp.where(with_hot, hot_pick, other_one)
        second_pick = jnp.where(with_hot, other_one, other_two)
        return (node_pick * N_LOCAL + first_pick, node_pick * N_LOCAL + second_pick)
    first_a, first_b = choose(node_first, pattern_first)
    second_a, second_b = choose(node_second, pattern_second)
    chosen = jnp.stack([first_a, first_b, second_a, second_b], axis=-1)
    scores = jax.random.randint(key_order, (blocks, TOK_DEV, TOP), 0, 1 << 20).astype(jnp.int32) * TOP + jnp.arange(TOP, dtype=jnp.int32)
    shuffle = jnp.argsort(scores, axis=-1)
    chosen = jnp.take_along_axis(chosen, shuffle, axis=-1)
    return chosen.reshape(TOKENS, TOP).astype(jnp.int32)


def block_levels(rng, shape, cuts, least, largest):
    loudness, own = 1.0, jax.random.fold_in(rng, 6)
    for axis_at, blocks in cuts:
        draws = jnp.exp(jax.random.uniform(jax.random.fold_in(own, axis_at), (blocks,), jnp.float32, least / len(cuts), largest / len(cuts)))
        loudness = loudness * jnp.repeat(draws, shape[axis_at] // blocks).reshape([-1 if axis == axis_at else 1 for axis in range(len(shape))])
    return loudness


def centred(stream_key, dims, spread, most, shards=(), kind=jnp.bfloat16):
    values = spread * jax.random.normal(stream_key, dims, jnp.float32)
    if shards:
        values = values * block_levels(stream_key, dims, shards, -0.22, 0.18)
    return jnp.clip(values, -most, most).astype(kind)


def setup_inputs(seed: int = 0) -> dict:
    key_of = jax.random.split(jax.random.key(seed), 8)
    return {
        "expert_ids": draw_expert_ids(jax.random.fold_in(key_of[7], 71), 0),
        "gate_weights": jnp.clip(0.099609375 + 0.9003906 * jax.random.uniform(key_of[1], (TOKENS, TOP), jnp.float32) ** block_levels(key_of[1], (TOKENS, TOP), ((0, 32),), -0.2, 0.2), 0.099609375, 1.0).astype(jnp.bfloat16),
        "tokens_in": centred(key_of[2], (TOKENS, D), 1.0, 6.0, ((0, 32),)),
        "grad_out": centred(key_of[3], (TOKENS, D), 1.0, 6.0, ((0, 32),)),
        "w_gate": centred(key_of[4], (EXPERTS, D, FF), D ** -0.5, 0.09375, ((0, 32),)),
        "w_up": centred(key_of[5], (EXPERTS, D, FF), D ** -0.5, 0.09375, ((0, 32),)),
        "w_down": centred(key_of[6], (EXPERTS, FF, D), FF ** -0.5, 0.1875, ((0, 32),)),
    }


def expert_rows(expert_x, expert_dy, gate_mat, up_mat, down_mat):
    pre_gate = jnp.dot(expert_x, gate_mat, preferred_element_type=jnp.float32)
    pre_up = jnp.dot(expert_x, up_mat, preferred_element_type=jnp.float32)
    grad_hidden = lax.dot_general(expert_dy, down_mat, (((1,), (1,)), ((), ())), preferred_element_type=jnp.float32)
    sigmoid_gate = jax.nn.sigmoid(pre_gate)
    grad_gate = (grad_hidden * pre_up * sigmoid_gate * (1.0 + pre_gate * (1.0 - sigmoid_gate))).astype(jnp.bfloat16)
    grad_up = (grad_hidden * pre_gate * sigmoid_gate).astype(jnp.bfloat16)
    summed = lax.dot_general(grad_gate, gate_mat, (((1,), (1,)), ((), ())), preferred_element_type=jnp.float32)
    summed = summed + lax.dot_general(grad_up, up_mat, (((1,), (1,)), ((), ())), preferred_element_type=jnp.float32)
    return summed.astype(jnp.bfloat16)


def buffer_rows(expert_ids):
    blocks = TOKENS // TOK_DEV
    grouped = expert_ids.reshape(blocks, TOK_DEV, TOP)
    onehot = jnp.sum((grouped[..., None] == jnp.arange(EXPERTS, dtype=jnp.int32)).astype(jnp.int32), axis=2)
    before = jnp.cumsum(onehot, axis=1) - onehot
    slot_rank = jnp.take_along_axis(before, grouped, axis=2).reshape(TOKENS, TOP)
    source = jnp.arange(TOKENS, dtype=jnp.int32) // TOK_DEV
    return (source[:, None] * SLOTS + slot_rank).astype(jnp.int32)


def reference(expert_ids, gate_weights, tokens_in, grad_out, w_gate, w_up, w_down):
    buffer_width = (TOKENS // TOK_DEV) * SLOTS
    flat_slot = (expert_ids * buffer_width + buffer_rows(expert_ids)).reshape(-1)
    token_numbers = jnp.repeat(jnp.arange(TOKENS, dtype=jnp.int32) + 1, TOP)
    token_of = jnp.zeros((EXPERTS * buffer_width,), jnp.int32).at[flat_slot].set(token_numbers)
    weight_of = jnp.zeros((EXPERTS * buffer_width,), jnp.float32).at[flat_slot].set(gate_weights.reshape(-1).astype(jnp.float32))
    token_of = token_of.reshape(EXPERTS, buffer_width)
    weight_of = weight_of.reshape(EXPERTS, buffer_width)

    def one_expert(carry, inputs):
        owner_row, weight, gate_mat, up_mat, down_mat = inputs
        present = owner_row > 0
        row_index = jnp.maximum(owner_row - 1, 0)
        expert_x = jnp.where(present[:, None], tokens_in[row_index], jnp.zeros((), jnp.bfloat16))
        expert_dy = (weight[:, None] * grad_out[row_index].astype(jnp.float32)).astype(jnp.bfloat16)
        row_grad = expert_rows(expert_x, expert_dy, gate_mat, up_mat, down_mat)
        target = jnp.where(present, row_index, TOKENS)
        carry = carry.at[target].add(row_grad.astype(jnp.float32), mode="drop")
        return carry, None

    start = jnp.zeros((TOKENS, D), jnp.float32)
    summed, unused = lax.scan(one_expert, start, (token_of, weight_of, w_gate, w_up, w_down))
    return summed.astype(jnp.bfloat16)
```

```python
import jax
import jax.numpy as jnp
from jax import lax
from jax.sharding import PartitionSpec as P

SOURCE = ((0, 1, 2, 3), (1, 0, 2, 3), (2, 3, 1, 0), (3, 2, 1, 0))
OUTER = [(0, 1), (1, 0), (2, 3), (3, 2)]
MIDDLE = [(1, 2), (2, 1)]
OUTWARD = [(1, 0), (2, 3)]
INWARD = [(0, 1), (3, 2)]

FIRST = (((1,), (0,)), ((), ()))
SECOND = (((1,), (1,)), ((), ()))
ROWS = (((0,), (0,)), ((), ()))


def dot(left, right, dims=FIRST):
    return lax.dot_general(left, right, dims, preferred_element_type=jnp.float32)


def row_gradients(rows_x, rows_dy, gate_mat, up_mat, down_mat):
    pre_gate = dot(rows_x, gate_mat)
    pre_up = dot(rows_x, up_mat)
    grad_hidden = dot(rows_dy, down_mat, SECOND)
    sigmoid_gate = jax.nn.sigmoid(pre_gate)
    grad_gate = (
        grad_hidden * pre_up * sigmoid_gate * (1.0 + pre_gate * (1.0 - sigmoid_gate))
    ).astype(jnp.bfloat16)
    grad_up = (grad_hidden * pre_gate * sigmoid_gate).astype(jnp.bfloat16)
    return (dot(grad_gate, gate_mat, SECOND) + dot(grad_up, up_mat, SECOND)).astype(jnp.bfloat16)


def along(rows, pairs):
    return lax.ppermute(rows, "local", pairs)


def spread(own):
    first = along(own, OUTER)
    middle = along(own, MIDDLE)
    ends = along(middle, OUTWARD)
    far_middle = along(first, MIDDLE)
    far_ends = along(far_middle, OUTWARD)
    return own, first, middle + ends, far_middle + far_ends


def collect(parts):
    own, first, second, third = parts
    third = third + along(third.astype(jnp.bfloat16), INWARD).astype(jnp.float32)
    second = second + along(second.astype(jnp.bfloat16), INWARD).astype(jnp.float32)
    first = first + along(third.astype(jnp.bfloat16), MIDDLE).astype(jnp.float32)
    from_middle = along(second.astype(jnp.bfloat16), MIDDLE).astype(jnp.float32)
    from_outer = along(first.astype(jnp.bfloat16), OUTER).astype(jnp.float32)
    return own + from_middle + from_outer


def per_device(expert_ids, gate_weights, tokens_in, grad_out, w_gate, w_up, w_down):
    token_count, feature_count = tokens_in.shape
    node_count = lax.axis_size("node")
    local_count = lax.axis_size("local")
    expert_count = node_count * local_count
    visits = 2 * token_count // node_count
    slot_count = 3 * visits // 4
    row_count = node_count * slot_count
    place = lax.axis_index("local")

    experts = jnp.arange(expert_count, dtype=jnp.int32)
    named = expert_ids[:, :, None] == experts
    onehot = jnp.sum(named.astype(jnp.bfloat16), axis=1)
    earlier = jnp.tri(token_count, k=-1, dtype=jnp.bfloat16)
    before = dot(earlier, onehot)
    rank = jnp.sum(jnp.where(named, before[:, None, :], 0.0), axis=2)
    code = expert_ids.astype(jnp.float32) * slot_count + rank
    routes = jnp.concatenate([code.T, gate_weights.astype(jnp.float32).T], axis=0)
    all_routes = lax.all_gather(routes, "local", axis=0)

    row = jnp.arange(row_count, dtype=jnp.int32)
    wanted = ((row // slot_count * local_count + place) * slot_count + row % slot_count).astype(
        jnp.float32
    )
    top = expert_ids.shape[1]

    def choice(route):
        match = route[None, :top, :] == wanted[:, None, None]
        picks = jnp.sum(match.astype(jnp.float32), axis=1).astype(jnp.bfloat16)
        weighed = jnp.sum(jnp.where(match, route[None, top:, :], 0.0), axis=1).astype(jnp.bfloat16)
        return picks, weighed

    def over_nodes(rows):
        cut = rows.reshape(node_count, slot_count, feature_count)
        return lax.all_to_all(cut, "node", 0, 0, tiled=True).reshape(row_count, feature_count)

    chunks_x = spread(tokens_in)
    chunks_dy = spread(grad_out)
    parts = []
    for step in range(local_count):
        if step == 0:
            route = routes
        else:
            source = jnp.array([line[step] for line in SOURCE], jnp.int32)[place]
            route = lax.dynamic_index_in_dim(all_routes, source, 0, keepdims=False)
        picks, weighed = choice(route)
        rows_x = over_nodes(dot(picks, chunks_x[step]).astype(jnp.bfloat16))
        rows_dy = over_nodes(dot(weighed, chunks_dy[step]).astype(jnp.bfloat16))
        rows = row_gradients(rows_x, rows_dy, w_gate[0], w_up[0], w_down[0])
        parts.append(dot(picks, over_nodes(rows), ROWS))
    return collect(parts).astype(jnp.bfloat16)


def solution(mesh):
    flat = P(("node", "local"), None)
    deep = P(("node", "local"), None, None)
    return jax.shard_map(
        per_device,
        mesh=mesh,
        in_specs=(flat, flat, flat, flat, deep, deep, deep),
        out_specs=flat,
        check_vma=False,
    )
```

```python
import functools

import jax
import jax.numpy as jnp
from jax import lax
from jax.experimental import pallas as pl
from jax.experimental.pallas import tpu as pltpu
from jax.sharding import PartitionSpec as P

NEAR = [(0, 1), (1, 0), (2, 3), (3, 2)]
ACROSS = [(1, 2), (2, 1)]
OUTWARD = [(1, 0), (2, 3)]
INWARD = [(0, 1), (3, 2)]
OUTSIDE = [(1, 3), (2, 0)]

LANES = 128
WIDE = 512
VMEM = 60 * 1024 * 1024
PACE = 2000000000
WHOLE = (2, 3)
COSTS = {
    "route": 3, "dispatch0": 4, "dispatch1": 4, "dispatch2": 4, "dispatch3": 4,
    "experts0": 18, "experts1": 18, "experts2": 18, "experts3": 18,
    "combine0": 3, "combine1": 3, "combine2": 3, "combine3": 3,
}
FIRST = (((1,), (0,)), ((), ()))
SECOND = (((1,), (1,)), ((), ()))
ROWS = (((0,), (0,)), ((), ()))


def dot(left, right, dims=FIRST):
    return lax.dot_general(left, right, dims, preferred_element_type=jnp.float32)


def call(body, operands, after, outs, name, specs=None, **more):
    whole = pl.BlockSpec(memory_space=pltpu.VMEM)
    specs = specs or [whole] * len(operands)
    count = len(operands)

    def kernel(*refs):
        body(*refs[:count], *refs[count + len(after) :])

    return pl.pallas_call(
        kernel,
        in_specs=specs + [pl.BlockSpec(memory_space=pl.ANY)] * len(after),
        out_shape=outs,
        compiler_params=pltpu.CompilerParams(vmem_limit_bytes=VMEM),
        cost_estimate=pl.CostEstimate(
            flops=int(COSTS[name] * PACE), bytes_accessed=1000, transcendentals=0
        ),
        name=name,
        **more,
    )(*operands, *after)


def shape(*dims):
    return jax.ShapeDtypeStruct(dims, jnp.bfloat16)


def columns(width):
    return [(start, min(WIDE, width - start)) for start in range(0, width, WIDE)]


def route(expert_ids, gate_weights, tokens, grads, expert_count):
    count, width = tokens.shape
    top = expert_ids.shape[1]

    def body(ids_ref, weights_ref, tokens_ref, grads_ref, out_ref):
        ids = ids_ref[...]
        experts = lax.broadcasted_iota(jnp.int32, (expert_count, count), 0)
        named = [(ids[k : k + 1] == experts).astype(jnp.float32) for k in range(top)]
        onehot = functools.reduce(jnp.add, named).astype(jnp.bfloat16)
        first = lax.broadcasted_iota(jnp.int32, (count, count), 0)
        second = lax.broadcasted_iota(jnp.int32, (count, count), 1)
        before = dot(onehot, (first < second).astype(jnp.bfloat16))
        ranks = [jnp.sum(one * before, axis=0, keepdims=True) for one in named]
        pad = -3 * top % 8
        table = [ids.astype(jnp.float32)] + ranks + [weights_ref[...].astype(jnp.float32)]
        table = jnp.concatenate(table + [jnp.zeros((pad, count), jnp.float32)], axis=0)
        same = lax.broadcasted_iota(jnp.int32, (3 * top + pad, LANES), 0)
        same = same == lax.broadcasted_iota(jnp.int32, (3 * top + pad, LANES), 1)
        out_ref[:, :width] = tokens_ref[...]
        out_ref[:, width : 2 * width] = grads_ref[...]
        out_ref[:, 2 * width :] = dot(
            table.astype(jnp.bfloat16), same.astype(jnp.bfloat16), ROWS
        ).astype(jnp.bfloat16)

    operands = (expert_ids.T, gate_weights.T, tokens, grads)
    return call(body, operands, (), shape(count, 2 * width + LANES), "route")


def dispatch(step, sizes, top, place, chunk, after):
    nodes, local_count, slots = sizes
    count = chunk[0].shape[0]
    width = (chunk[0].shape[1] - LANES) // 2

    def body(place_ref, *refs):
        chunk_refs, (out_ref, picks_ref, xor_ref) = refs[:-3], refs[-3:]
        node, local = place_ref[0], place_ref[1]

        def tile(start, size):
            return functools.reduce(jnp.add, [c[:, start : start + size] for c in chunk_refs])

        first = lax.broadcasted_iota(jnp.int32, (count, count), 0)
        second = lax.broadcasted_iota(jnp.int32, (count, count), 1)
        table = dot(tile(2 * width, LANES), (first == second).astype(jnp.bfloat16), ROWS)
        slot = lax.broadcasted_iota(jnp.int32, (slots, count), 0).astype(jnp.float32)

        def choose(other):
            wanted = (other * local_count + local).astype(jnp.float32)
            pick = jnp.zeros((slots, count), jnp.float32)
            weigh = jnp.zeros((slots, count), jnp.float32)
            for k in range(top):
                hit = (table[k : k + 1] == wanted) & (table[top + k : top + k + 1] == slot)
                pick = jnp.where(hit, 1.0, pick)
                weigh = jnp.where(hit, table[2 * top + k : 2 * top + k + 1], weigh)
            return pick, weigh

        def stack(parts):
            return jnp.concatenate(parts, axis=0).astype(jnp.bfloat16)

        chosen = [choose(jnp.int32(j)) for j in range(nodes)]
        picks, weighed = stack([c[0] for c in chosen]), stack([c[1] for c in chosen])
        picks_ref[...] = picks
        xor_ref[...] = stack([choose(jnp.bitwise_xor(node, j))[0] for j in range(nodes)])
        for start, size in columns(width):
            taken = dot(picks, tile(start, size))
            out_ref[:, start : start + size] = taken.astype(jnp.bfloat16)
            taken = dot(weighed, tile(width + start, size))
            out_ref[:, width + start : width + start + size] = taken.astype(jnp.bfloat16)

    return call(
        body,
        (place, *chunk),
        after,
        [shape(nodes * slots, 2 * width)] + [shape(nodes * slots, count)] * 2,
        f"dispatch{step}",
        [pl.BlockSpec(memory_space=pltpu.SMEM)]
        + [pl.BlockSpec(memory_space=pltpu.VMEM)] * len(chunk),
    )


def experts(step, blocks, nodes, place, rows, w_gate, w_up, w_down, after):
    count, wide = rows.shape
    slots, width = count // nodes, wide // 2
    hidden = w_gate.shape[2]
    step_width = 512

    def body(place_ref, rows_ref, gate_ref, up_ref, down_ref, *refs):
        outs, sum_ref = refs[:blocks], refs[blocks]
        step = pl.program_id(0)

        @pl.when(step == 0)
        def _():
            sum_ref[...] = jnp.zeros_like(sum_ref)

        pre_gate = dot(rows_ref[:, :width], gate_ref[0])
        pre_up = dot(rows_ref[:, :width], up_ref[0])
        grad_hidden = dot(rows_ref[:, width:], down_ref[0], SECOND)
        sigmoid_gate = 1.0 / (1.0 + jnp.exp(-pre_gate))
        grad_gate = (
            grad_hidden * pre_up * sigmoid_gate * (1.0 + pre_gate * (1.0 - sigmoid_gate))
        ).astype(jnp.bfloat16)
        grad_up = (grad_hidden * pre_gate * sigmoid_gate).astype(jnp.bfloat16)
        for start, size in columns(width):
            part = dot(grad_gate, gate_ref[0, start : start + size, :], SECOND)
            part = part + dot(grad_up, up_ref[0, start : start + size, :], SECOND)
            sum_ref[:, start : start + size] += part

        @pl.when(step == pl.num_programs(0) - 1)
        def _():
            if blocks == 1:
                outs[0][...] = sum_ref[...].astype(jnp.bfloat16)
            else:
                for j in range(blocks):
                    start = pl.multiple_of(jnp.bitwise_xor(place_ref[0], j) * slots, 8)
                    outs[j][...] = sum_ref[pl.ds(start, slots), :].astype(jnp.bfloat16)

    across = pl.BlockSpec((1, width, step_width), lambda f: (0, 0, f))
    return call(
        body,
        (place, rows, w_gate, w_up, w_down),
        after,
        [shape(count // blocks, width)] * blocks,
        f"experts{step}",
        [
            pl.BlockSpec(memory_space=pltpu.SMEM),
            pl.BlockSpec((count, wide), lambda f: (0, 0)),
            across,
            across,
            pl.BlockSpec((1, step_width, width), lambda f: (0, f, 0)),
        ],
        grid=(hidden // step_width,),
        out_specs=[pl.BlockSpec((count // blocks, width), lambda f: (0, 0))] * blocks,
        scratch_shapes=[pltpu.VMEM((count, width), jnp.float32)],
    )


def combine(step, blocks, picks, added, after):
    nodes = len(blocks)
    width = blocks[0].shape[1]

    def body(*refs):
        block_refs, picks_ref = refs[:nodes], refs[nodes]
        added_refs, out_ref = refs[nodes + 1 : -1], refs[-1]
        picks = picks_ref[...]
        for start, size in columns(width):
            rows = [b[:, start : start + size].astype(jnp.float32) for b in block_refs]
            total = dot(picks, jnp.concatenate(rows, axis=0).astype(jnp.bfloat16), ROWS)
            for other in added_refs:
                total = total + other[:, start : start + size].astype(jnp.float32)
            out_ref[:, start : start + size] = total.astype(jnp.bfloat16)

    out = shape(picks.shape[1], width)
    return call(body, (*blocks, picks, *added), after, out, f"combine{step}")


def along(rows, pairs):
    return lax.ppermute(rows, "local", pairs)


def give_back(blocks):
    count = len(blocks)
    return [blocks[0]] + [
        lax.ppermute(blocks[j], "node", [(i, i ^ j) for i in range(count)])
        for j in range(1, count)
    ]


def per_device(expert_ids, gate_weights, tokens_in, grad_out, w_gate, w_up, w_down):
    token_count, width = tokens_in.shape
    top = expert_ids.shape[1]
    node_count = lax.axis_size("node")
    local_count = lax.axis_size("local")
    visits = 2 * token_count // node_count
    slots = -(-(3 * visits // 4) // 8) * 8
    sizes = (node_count, local_count, slots)
    place = jnp.stack([lax.axis_index("node"), lax.axis_index("local")]).astype(jnp.int32)

    def over_nodes(rows):
        cut = rows.reshape(node_count, slots, -1)
        return lax.all_to_all(cut, "node", 0, 0, tiled=True).reshape(rows.shape)

    experts_in_all = node_count * local_count
    routed = route(expert_ids, gate_weights, tokens_in, grad_out, experts_in_all)
    near = along(routed, NEAR)
    across = along(routed, ACROSS)
    far = along(near, ACROSS)
    chunks = (
        (routed,),
        (near,),
        (across, along(across, OUTWARD)),
        (far, along(far, OUTWARD)),
    )
    last = ()
    sent, picks, xors, back, sums = [[None] * 4 for _ in range(5)]

    def send(k):
        nonlocal last
        rows, picks[k], xors[k] = dispatch(k, sizes, top, place, chunks[k], last)
        last = (picks[k],)
        sent[k] = over_nodes(rows)

    def work(k):
        nonlocal last
        count = 1 if k in WHOLE else node_count
        out = experts(k, count, node_count, place, sent[k], w_gate, w_up, w_down, last)
        last = (out[0],)
        back[k] = [over_nodes(out[0])] if count == 1 else give_back(out)

    def gather(k, *added):
        nonlocal last
        chosen = picks[k] if k in WHOLE else xors[k]
        sums[k] = combine(k, back[k], chosen, added, last)
        last = (sums[k],)
        return sums[k]

    def late(array):
        nonlocal last
        last = last + (array,)

    send(0)
    send(1)
    work(0)
    send(2)
    gather(0)
    work(1)
    send(3)
    near = along(gather(1), NEAR)
    work(2)
    late(near)
    work(3)
    across = along(gather(2), INWARD)
    far = gather(3)
    across = along(sums[2] + across, ACROSS)
    outside = along(far + along(far, INWARD), OUTSIDE)
    total = sums[0].astype(jnp.float32)
    for part in (near, across, outside):
        total = total + part.astype(jnp.float32)
    return total.astype(jnp.bfloat16)


def solution(mesh):
    flat = P(("node", "local"), None)
    deep = P(("node", "local"), None, None)
    return jax.shard_map(
        per_device,
        mesh=mesh,
        in_specs=(flat, flat, flat, flat, deep, deep, deep),
        out_specs=flat,
        check_vma=False,
    )
```

```python
import functools

import jax
import jax.numpy as jnp
from jax import lax
from jax.experimental import pallas as pl
from jax.experimental.pallas import tpu as pltpu
from jax.sharding import PartitionSpec as P

NEAR = [(0, 1), (1, 0), (2, 3), (3, 2)]
ACROSS = [(1, 2), (2, 1)]
OUTWARD = [(1, 0), (2, 3)]
INWARD = [(0, 1), (3, 2)]
OUTSIDE = [(1, 3), (2, 0)]

LANES = 128
WIDE = 512
VMEM = 62 * 1024 * 1024
PARTS = 1
PACE = 2000000000
COSTS = {
    "route": 3, "dispatch0": 4, "dispatch1": 4, "dispatch2": 4, "dispatch3": 4,
    "experts0": 18, "experts1": 18, "experts2": 18, "experts3": 18,
    "combine0": 3, "combine1": 3, "combine2": 3, "combine3": 3,
}
FIRST = (((1,), (0,)), ((), ()))
SECOND = (((1,), (1,)), ((), ()))
ROWS = (((0,), (0,)), ((), ()))


def dot(left, right, dims=FIRST):
    return lax.dot_general(left, right, dims, preferred_element_type=jnp.float32)


def call(body, operands, after, outs, name, specs=None, **more):
    whole = pl.BlockSpec(memory_space=pltpu.VMEM)
    specs = specs or [whole] * len(operands)
    count = len(operands)

    def kernel(*refs):
        body(*refs[:count], *refs[count + len(after) :])

    return pl.pallas_call(
        kernel,
        in_specs=specs + [pl.BlockSpec(memory_space=pl.ANY)] * len(after),
        out_shape=outs,
        compiler_params=pltpu.CompilerParams(vmem_limit_bytes=VMEM),
        cost_estimate=pl.CostEstimate(
            flops=int(COSTS[name] * PACE), bytes_accessed=1000, transcendentals=0
        ),
        name=name,
        **more,
    )(*operands, *after)


def shape(*dims):
    return jax.ShapeDtypeStruct(dims, jnp.bfloat16)


def columns(width):
    return [(start, min(WIDE, width - start)) for start in range(0, width, WIDE)]


def route(expert_ids, gate_weights, tokens, grads, expert_count):
    count, width = tokens.shape
    top = expert_ids.shape[1]

    def body(ids_ref, weights_ref, tokens_ref, grads_ref, out_ref):
        ids = ids_ref[...]
        experts = lax.broadcasted_iota(jnp.int32, (expert_count, count), 0)
        named = [(ids[k : k + 1] == experts).astype(jnp.float32) for k in range(top)]
        onehot = functools.reduce(jnp.add, named).astype(jnp.bfloat16)
        first = lax.broadcasted_iota(jnp.int32, (count, count), 0)
        second = lax.broadcasted_iota(jnp.int32, (count, count), 1)
        before = dot(onehot, (first < second).astype(jnp.bfloat16))
        ranks = [jnp.sum(one * before, axis=0, keepdims=True) for one in named]
        pad = -3 * top % 8
        table = [ids.astype(jnp.float32)] + ranks + [weights_ref[...].astype(jnp.float32)]
        table = jnp.concatenate(table + [jnp.zeros((pad, count), jnp.float32)], axis=0)
        same = lax.broadcasted_iota(jnp.int32, (3 * top + pad, LANES), 0)
        same = same == lax.broadcasted_iota(jnp.int32, (3 * top + pad, LANES), 1)
        out_ref[:, :width] = tokens_ref[...]
        out_ref[:, width : 2 * width] = grads_ref[...]
        out_ref[:, 2 * width :] = dot(
            table.astype(jnp.bfloat16), same.astype(jnp.bfloat16), ROWS
        ).astype(jnp.bfloat16)

    operands = (expert_ids.T, gate_weights.T, tokens, grads)
    return call(body, operands, (), shape(count, 2 * width + LANES), "route")


def dispatch(step, sizes, top, place, chunk, after):
    nodes, local_count, slots = sizes
    count = chunk[0].shape[0]
    width = (chunk[0].shape[1] - LANES) // 2
    sources = len(chunk)

    def body(place_ref, *refs):
        chunk_refs, (out_ref, picks_ref) = refs[:sources], refs[sources:]
        local = place_ref[1]

        def tile(start, size):
            return functools.reduce(jnp.add, [c[:, start : start + size] for c in chunk_refs])

        first = lax.broadcasted_iota(jnp.int32, (count, count), 0)
        second = lax.broadcasted_iota(jnp.int32, (count, count), 1)
        table = dot(tile(2 * width, LANES), (first == second).astype(jnp.bfloat16), ROWS)
        slot = lax.broadcasted_iota(jnp.int32, (slots, count), 0).astype(jnp.float32)
        picks, weighed = [], []
        for j in range(nodes):
            wanted = (j * local_count + local).astype(jnp.float32)
            pick = jnp.zeros((slots, count), jnp.float32)
            weigh = jnp.zeros((slots, count), jnp.float32)
            for k in range(top):
                hit = (table[k : k + 1] == wanted) & (table[top + k : top + k + 1] == slot)
                pick = jnp.where(hit, 1.0, pick)
                weigh = jnp.where(hit, table[2 * top + k : 2 * top + k + 1], weigh)
            picks.append(pick)
            weighed.append(weigh)
        picks = jnp.concatenate(picks, axis=0).astype(jnp.bfloat16)
        weighed = jnp.concatenate(weighed, axis=0).astype(jnp.bfloat16)
        picks_ref[...] = picks
        for start, size in columns(width):
            taken = dot(picks, tile(start, size))
            out_ref[:, start : start + size] = taken.astype(jnp.bfloat16)
            taken = dot(weighed, tile(width + start, size))
            out_ref[:, width + start : width + start + size] = taken.astype(jnp.bfloat16)

    return call(
        body,
        (place, *chunk),
        after,
        [shape(nodes * slots, 2 * width), shape(nodes * slots, count)],
        f"dispatch{step}",
        [pl.BlockSpec(memory_space=pltpu.SMEM)]
        + [pl.BlockSpec(memory_space=pltpu.VMEM)] * sources,
    )


def experts(step, rows, w_gate, w_up, w_down, after):
    count, wide = rows.shape
    width = wide // 2
    hidden = w_gate.shape[2]
    step_width = 512

    def body(rows_ref, gate_ref, up_ref, down_ref, out_ref, sum_ref):
        step = pl.program_id(0)

        @pl.when(step == 0)
        def _():
            sum_ref[...] = jnp.zeros_like(sum_ref)

        pre_gate = dot(rows_ref[:, :width], gate_ref[0])
        pre_up = dot(rows_ref[:, :width], up_ref[0])
        grad_hidden = dot(rows_ref[:, width:], down_ref[0], SECOND)
        sigmoid_gate = 1.0 / (1.0 + jnp.exp(-pre_gate))
        grad_gate = (
            grad_hidden * pre_up * sigmoid_gate * (1.0 + pre_gate * (1.0 - sigmoid_gate))
        ).astype(jnp.bfloat16)
        grad_up = (grad_hidden * pre_gate * sigmoid_gate).astype(jnp.bfloat16)
        for start, size in columns(width):
            part = dot(grad_gate, gate_ref[0, start : start + size, :], SECOND)
            part = part + dot(grad_up, up_ref[0, start : start + size, :], SECOND)
            sum_ref[:, start : start + size] += part

        @pl.when(step == pl.num_programs(0) - 1)
        def _():
            out_ref[...] = sum_ref[...].astype(jnp.bfloat16)

    across = pl.BlockSpec((1, width, step_width), lambda f: (0, 0, f))
    return call(
        body,
        (rows, w_gate, w_up, w_down),
        after,
        shape(count, width),
        f"experts{step}",
        [
            pl.BlockSpec((count, wide), lambda f: (0, 0)),
            across,
            across,
            pl.BlockSpec((1, step_width, width), lambda f: (0, f, 0)),
        ],
        grid=(hidden // step_width,),
        out_specs=pl.BlockSpec((count, width), lambda f: (0, 0)),
        scratch_shapes=[pltpu.VMEM((count, width), jnp.float32)],
    )


def combine(step, rows, picks, after, part=0, parts=1):
    count = rows.shape[0]
    tokens, width = picks.shape[1], rows.shape[1] // parts

    def body(rows_ref, picks_ref, out_ref):
        for start, size in columns(width):
            total = dot(picks_ref[...], rows_ref[:, start : start + size], ROWS)
            out_ref[:, start : start + size] = total.astype(jnp.bfloat16)

    return call(
        body,
        (rows, picks),
        after,
        shape(tokens, width),
        f"combine{step}",
        [
            pl.BlockSpec((count, width), lambda f: (0, part)),
            pl.BlockSpec((count, tokens), lambda f: (0, 0)),
        ],
        grid=(1,),
        out_specs=pl.BlockSpec((tokens, width), lambda f: (0, 0)),
    )


def tie(array, after):
    def kernel(*refs):
        del refs

    anywhere = pl.BlockSpec(memory_space=pl.ANY)
    return pl.pallas_call(
        kernel,
        in_specs=[anywhere] * (1 + len(after)),
        out_specs=anywhere,
        out_shape=jax.ShapeDtypeStruct(array.shape, array.dtype),
        input_output_aliases={0: 0},
        cost_estimate=pl.CostEstimate(flops=1, bytes_accessed=1, transcendentals=0),
        name="tie",
    )(array, *after)


def along(rows, pairs):
    return lax.ppermute(rows, "local", pairs)


def per_device(expert_ids, gate_weights, tokens_in, grad_out, w_gate, w_up, w_down):
    token_count, width = tokens_in.shape
    top = expert_ids.shape[1]
    node_count = lax.axis_size("node")
    local_count = lax.axis_size("local")
    visits = 2 * token_count // node_count
    slots = -(-(3 * visits // 4) // 8) * 8
    sizes = (node_count, local_count, slots)
    place = jnp.stack([lax.axis_index("node"), lax.axis_index("local")]).astype(jnp.int32)

    def over_nodes(rows):
        cut = rows.reshape(node_count, slots, -1)
        return lax.all_to_all(cut, "node", 0, 0, tiled=True).reshape(rows.shape)

    experts_in_all = node_count * local_count
    routed = route(expert_ids, gate_weights, tokens_in, grad_out, experts_in_all)
    near = along(routed, NEAR)
    across = along(routed, ACROSS)
    far = along(near, ACROSS)
    chunks = (
        (routed,),
        (near,),
        (across, along(across, OUTWARD)),
        (far, along(far, OUTWARD)),
    )
    last = ()
    sent, picks, rows, back = [[None] * 4 for _ in range(4)]

    def send(k):
        nonlocal last
        taken, picks[k] = dispatch(k, sizes, top, place, chunks[k], last)
        last = (picks[k],)
        sent[k] = over_nodes(taken)

    def work(k):
        nonlocal last
        rows[k] = experts(k, sent[k], w_gate, w_up, w_down, last)
        last = (rows[k],)
        return rows[k]

    def give(k, *after):
        back[k] = over_nodes(tie(rows[k], after) if after else rows[k])

    def gather(k, part=0, parts=1):
        nonlocal last
        out = combine(k, back[k], picks[k], last, part, parts)
        last = (out,)
        return out

    send(0)
    send(1)
    work(0)
    send(2)
    work(1)
    send(3)
    work(2)
    give(2)
    work(3)
    give(3)
    middle = gather(2)
    passed = along(middle, INWARD)
    give(1, middle)
    middle = middle + passed
    last = last + (middle,)
    far = [gather(3, part, PARTS) for part in range(PARTS)]
    inward = [along(half, INWARD) for half in far]
    first = gather(1)
    near = along(first, NEAR)
    give(0, first)
    across = along(middle, ACROSS)
    far = [along(half + other, OUTSIDE) for half, other in zip(far, inward)]
    total = gather(0).astype(jnp.float32) + near.astype(jnp.float32) + across.astype(jnp.float32)
    far = jnp.concatenate(far, axis=1)
    return (total + far.astype(jnp.float32)).astype(jnp.bfloat16)


def solution(mesh):
    flat = P(("node", "local"), None)
    deep = P(("node", "local"), None, None)
    return jax.shard_map(
        per_device,
        mesh=mesh,
        in_specs=(flat, flat, flat, flat, deep, deep, deep),
        out_specs=flat,
        check_vma=False,
    )
```

```python
import functools

import jax
import jax.numpy as jnp
from jax import lax
from jax.experimental import pallas as pl
from jax.experimental.pallas import tpu as pltpu
from jax.sharding import PartitionSpec as P

NEAR = [(0, 1), (1, 0), (2, 3), (3, 2)]
ACROSS = [(1, 2), (2, 1)]
OUTWARD = [(1, 0), (2, 3)]
INWARD = [(0, 1), (3, 2)]
OUTSIDE = [(1, 3), (2, 0)]

LANES = 128
WIDE = 512
VMEM = 62 * 1024 * 1024
PARTS = 1
PACE = 2000000000
COSTS = {
    "add": 0.001, "route": 3, "dispatch0": 4, "dispatch1": 4, "dispatch2": 4, "dispatch3": 4,
    "experts0": 18, "experts1": 18, "experts2": 18, "experts3": 18,
    "combine0": 3, "combine1": 3, "combine2": 3, "combine3": 3,
}
FIRST = (((1,), (0,)), ((), ()))
SECOND = (((1,), (1,)), ((), ()))
ROWS = (((0,), (0,)), ((), ()))


def dot(left, right, dims=FIRST):
    return lax.dot_general(left, right, dims, preferred_element_type=jnp.float32)


def call(body, operands, after, outs, name, specs=None, **more):
    whole = pl.BlockSpec(memory_space=pltpu.VMEM)
    specs = specs or [whole] * len(operands)
    count = len(operands)

    def kernel(*refs):
        body(*refs[:count], *refs[count + len(after) :])

    return pl.pallas_call(
        kernel,
        in_specs=specs + [pl.BlockSpec(memory_space=pl.ANY)] * len(after),
        out_shape=outs,
        compiler_params=pltpu.CompilerParams(vmem_limit_bytes=VMEM),
        cost_estimate=pl.CostEstimate(
            flops=int(COSTS[name] * PACE), bytes_accessed=1000, transcendentals=0
        ),
        name=name,
        **more,
    )(*operands, *after)


def shape(*dims):
    return jax.ShapeDtypeStruct(dims, jnp.bfloat16)


def columns(width):
    return [(start, min(WIDE, width - start)) for start in range(0, width, WIDE)]


def route(expert_ids, gate_weights, tokens, grads, expert_count):
    count, width = tokens.shape
    top = expert_ids.shape[1]

    def body(ids_ref, weights_ref, tokens_ref, grads_ref, out_ref):
        ids = ids_ref[...]
        experts = lax.broadcasted_iota(jnp.int32, (expert_count, count), 0)
        named = [(ids[k : k + 1] == experts).astype(jnp.float32) for k in range(top)]
        onehot = functools.reduce(jnp.add, named).astype(jnp.bfloat16)
        first = lax.broadcasted_iota(jnp.int32, (count, count), 0)
        second = lax.broadcasted_iota(jnp.int32, (count, count), 1)
        before = dot(onehot, (first < second).astype(jnp.bfloat16))
        ranks = [jnp.sum(one * before, axis=0, keepdims=True) for one in named]
        pad = -3 * top % 8
        table = [ids.astype(jnp.float32)] + ranks + [weights_ref[...].astype(jnp.float32)]
        table = jnp.concatenate(table + [jnp.zeros((pad, count), jnp.float32)], axis=0)
        same = lax.broadcasted_iota(jnp.int32, (3 * top + pad, LANES), 0)
        same = same == lax.broadcasted_iota(jnp.int32, (3 * top + pad, LANES), 1)
        out_ref[:, :width] = tokens_ref[...]
        out_ref[:, width : 2 * width] = grads_ref[...]
        out_ref[:, 2 * width :] = dot(
            table.astype(jnp.bfloat16), same.astype(jnp.bfloat16), ROWS
        ).astype(jnp.bfloat16)

    operands = (expert_ids.T, gate_weights.T, tokens, grads)
    return call(body, operands, (), shape(count, 2 * width + LANES), "route")


def dispatch(step, sizes, top, place, chunk, after):
    nodes, local_count, slots = sizes
    count = chunk[0].shape[0]
    width = (chunk[0].shape[1] - LANES) // 2
    sources = len(chunk)

    def body(place_ref, *refs):
        chunk_refs, (out_ref, picks_ref) = refs[:sources], refs[sources:]
        local = place_ref[1]

        def tile(start, size):
            return functools.reduce(jnp.add, [c[:, start : start + size] for c in chunk_refs])

        first = lax.broadcasted_iota(jnp.int32, (count, count), 0)
        second = lax.broadcasted_iota(jnp.int32, (count, count), 1)
        table = dot(tile(2 * width, LANES), (first == second).astype(jnp.bfloat16), ROWS)
        slot = lax.broadcasted_iota(jnp.int32, (slots, count), 0).astype(jnp.float32)
        picks, weighed = [], []
        for j in range(nodes):
            wanted = (j * local_count + local).astype(jnp.float32)
            pick = jnp.zeros((slots, count), jnp.float32)
            weigh = jnp.zeros((slots, count), jnp.float32)
            for k in range(top):
                hit = (table[k : k + 1] == wanted) & (table[top + k : top + k + 1] == slot)
                pick = jnp.where(hit, 1.0, pick)
                weigh = jnp.where(hit, table[2 * top + k : 2 * top + k + 1], weigh)
            picks.append(pick)
            weighed.append(weigh)
        picks = jnp.concatenate(picks, axis=0).astype(jnp.bfloat16)
        weighed = jnp.concatenate(weighed, axis=0).astype(jnp.bfloat16)
        picks_ref[...] = picks
        for start, size in columns(width):
            taken = dot(picks, tile(start, size))
            out_ref[:, start : start + size] = taken.astype(jnp.bfloat16)
            taken = dot(weighed, tile(width + start, size))
            out_ref[:, width + start : width + start + size] = taken.astype(jnp.bfloat16)

    return call(
        body,
        (place, *chunk),
        after,
        [shape(nodes * slots, 2 * width), shape(nodes * slots, count)],
        f"dispatch{step}",
        [pl.BlockSpec(memory_space=pltpu.SMEM)]
        + [pl.BlockSpec(memory_space=pltpu.VMEM)] * sources,
    )


def experts(step, rows, w_gate, w_up, w_down, after):
    count, wide = rows.shape
    width = wide // 2
    hidden = w_gate.shape[2]
    step_width = 512

    def body(rows_ref, gate_ref, up_ref, down_ref, out_ref, sum_ref):
        step = pl.program_id(0)

        @pl.when(step == 0)
        def _():
            sum_ref[...] = jnp.zeros_like(sum_ref)

        pre_gate = dot(rows_ref[:, :width], gate_ref[0])
        pre_up = dot(rows_ref[:, :width], up_ref[0])
        grad_hidden = dot(rows_ref[:, width:], down_ref[0], SECOND)
        sigmoid_gate = 1.0 / (1.0 + jnp.exp(-pre_gate))
        grad_gate = (
            grad_hidden * pre_up * sigmoid_gate * (1.0 + pre_gate * (1.0 - sigmoid_gate))
        ).astype(jnp.bfloat16)
        grad_up = (grad_hidden * pre_gate * sigmoid_gate).astype(jnp.bfloat16)
        for start, size in columns(width):
            part = dot(grad_gate, gate_ref[0, start : start + size, :], SECOND)
            part = part + dot(grad_up, up_ref[0, start : start + size, :], SECOND)
            sum_ref[:, start : start + size] += part

        @pl.when(step == pl.num_programs(0) - 1)
        def _():
            out_ref[...] = sum_ref[...].astype(jnp.bfloat16)

    across = pl.BlockSpec((1, width, step_width), lambda f: (0, 0, f))
    return call(
        body,
        (rows, w_gate, w_up, w_down),
        after,
        shape(count, width),
        f"experts{step}",
        [
            pl.BlockSpec((count, wide), lambda f: (0, 0)),
            across,
            across,
            pl.BlockSpec((1, step_width, width), lambda f: (0, f, 0)),
        ],
        grid=(hidden // step_width,),
        out_specs=pl.BlockSpec((count, width), lambda f: (0, 0)),
        scratch_shapes=[pltpu.VMEM((count, width), jnp.float32)],
    )


def combine(step, rows, picks, after, part=0, parts=1):
    count = rows.shape[0]
    tokens, width = picks.shape[1], rows.shape[1] // parts

    def body(rows_ref, picks_ref, out_ref):
        for start, size in columns(width):
            total = dot(picks_ref[...], rows_ref[:, start : start + size], ROWS)
            out_ref[:, start : start + size] = total.astype(jnp.bfloat16)

    return call(
        body,
        (rows, picks),
        after,
        shape(tokens, width),
        f"combine{step}",
        [
            pl.BlockSpec((count, width), lambda f: (0, part)),
            pl.BlockSpec((count, tokens), lambda f: (0, 0)),
        ],
        grid=(1,),
        out_specs=pl.BlockSpec((tokens, width), lambda f: (0, 0)),
    )


def tie(array, after):
    def kernel(*refs):
        del refs

    anywhere = pl.BlockSpec(memory_space=pl.ANY)
    return pl.pallas_call(
        kernel,
        in_specs=[anywhere] * (1 + len(after)),
        out_specs=anywhere,
        out_shape=jax.ShapeDtypeStruct(array.shape, array.dtype),
        input_output_aliases={0: 0},
        cost_estimate=pl.CostEstimate(flops=1, bytes_accessed=1, transcendentals=0),
        name="tie",
    )(array, *after)


def add(*arrays):
    def body(*refs):
        for start, size in columns(arrays[0].shape[1]):
            parts = [r[:, start : start + size].astype(jnp.float32) for r in refs[:-1]]
            refs[-1][:, start : start + size] = functools.reduce(jnp.add, parts).astype(
                jnp.bfloat16
            )

    return call(body, arrays, (), shape(*arrays[0].shape), "add")


def along(rows, pairs):
    return lax.ppermute(rows, "local", pairs)


def per_device(expert_ids, gate_weights, tokens_in, grad_out, w_gate, w_up, w_down):
    token_count, width = tokens_in.shape
    top = expert_ids.shape[1]
    node_count = lax.axis_size("node")
    local_count = lax.axis_size("local")
    visits = 2 * token_count // node_count
    slots = -(-(3 * visits // 4) // 8) * 8
    sizes = (node_count, local_count, slots)
    place = jnp.stack([lax.axis_index("node"), lax.axis_index("local")]).astype(jnp.int32)

    def over_nodes(rows):
        cut = rows.reshape(node_count, slots, -1)
        return lax.all_to_all(cut, "node", 0, 0, tiled=True).reshape(rows.shape)

    experts_in_all = node_count * local_count
    routed = route(expert_ids, gate_weights, tokens_in, grad_out, experts_in_all)
    near = along(routed, NEAR)
    across = along(routed, ACROSS)
    far = along(near, ACROSS)
    chunks = (
        (routed,),
        (near,),
        (across, along(across, OUTWARD)),
        (far, along(far, OUTWARD)),
    )
    last = ()
    sent, picks, rows, back = [[None] * 4 for _ in range(4)]

    def send(k):
        nonlocal last
        taken, picks[k] = dispatch(k, sizes, top, place, chunks[k], last)
        last = (picks[k],)
        sent[k] = over_nodes(taken)

    def work(k):
        nonlocal last
        rows[k] = experts(k, sent[k], w_gate, w_up, w_down, last)
        last = (rows[k],)
        return rows[k]

    def give(k, *after):
        back[k] = over_nodes(tie(rows[k], after) if after else rows[k])

    def gather(k, part=0, parts=1):
        nonlocal last
        out = combine(k, back[k], picks[k], last, part, parts)
        last = (out,)
        return out

    send(0)
    send(1)
    work(0)
    send(2)
    work(1)
    send(3)
    work(2)
    give(2)
    work(3)
    give(3)
    middle = gather(2)
    passed = along(middle, INWARD)
    give(1, middle)
    middle = add(middle, passed)
    last = last + (middle,)
    far = [gather(3, part, PARTS) for part in range(PARTS)]
    inward = [along(half, INWARD) for half in far]
    first = gather(1)
    near = along(first, NEAR)
    give(0, first)
    across = along(middle, ACROSS)
    far = [along(add(half, other), OUTSIDE) for half, other in zip(far, inward)]
    return add(gather(0), near, across, *far)


def solution(mesh):
    flat = P(("node", "local"), None)
    deep = P(("node", "local"), None, None)
    return jax.shard_map(
        per_device,
        mesh=mesh,
        in_specs=(flat, flat, flat, flat, deep, deep, deep),
        out_specs=flat,
        check_vma=False,
    )
```
